32 devices in a mesh: dp: 32 (over z, y, x, core).
Axes of the slice: x: 2, y: 2, z: 4, core: 2. Of those that a mesh axis runs over, the one named last changes fastest.
Arguments:
- residual_in: bfloat16 [12288, 1024], P('dp'), may hold values from -6 to 6
- cotangent: bfloat16 [12288, 1024], P('dp'), may hold values from -6 to 6
- seq_lengths: int32 [8], replicated, may hold values from 768 to 3072, as said below
- mixer_master: float32 [1024, 6144], P('dp')
- mixer_moment: float32 [1024, 6144], P('dp')
- mixer_square: float32 [1024, 6144], P('dp')
- dense_master: float32 [1024, 9216], P('dp')
- dense_moment: float32 [1024, 9216], P('dp')
- dense_square: float32 [1024, 9216], P('dp')
- gains_master: float32 [2304], P('dp')
- gains_moment: float32 [2304], P('dp')
- gains_square: float32 [2304], P('dp')
Outputs:
- block_output: bfloat16 [12288, 1024], P('dp')
- residual_grad: float32 [12288, 1024], P('dp')
- mixer_renewed: float32 [1024, 6144], P('dp')
- mixer_momentum: float32 [1024, 6144], P('dp')
- mixer_variance: float32 [1024, 6144], P('dp')
- dense_renewed: float32 [1024, 9216], P('dp')
- dense_momentum: float32 [1024, 9216], P('dp')
- dense_variance: float32 [1024, 9216], P('dp')
- gains_renewed: float32 [2304], P('dp')
- gains_momentum: float32 [2304], P('dp')
- gains_variance: float32 [2304], P('dp')
The draws below stay inside these ranges and needn't reach their ends.
Inputs may be any that keep to these rules, and one draw needn't show every extreme that they name: `seq_lengths`: they sum to 12288, and one of them equals 3072.
All inputs are finite; a program needn't handle non-finite values.
Results may differ from the reference program's by a relative error of at most 0.012.
The reference program's roundings to bfloat16 on the way count: a program that leaves them out, or rounds other values in their place, can miss the bound.
Values may be sent and summed in bfloat16 or wider, within the bound.
A program may use at most 256 MiB of HBM per device.

```python
import jax
import jax.numpy as jnp
from jax import lax

MODEL_WIDTH = 1024
QUERY_HEADS = 16
KEY_VALUE_HEADS = 8
HEAD_SIZE = 128
FF = 3072
TOK_DEV = 384
NSHIFT = 8
STEP = 10
TOKEN_COUNT = 12288
SEQS = 8
MAX_LEN = 3072
SHORTEST_LENGTH = 768
MIXER_COLUMNS = 6144
DENSE_COLS = 9216
GAINS = 2304


def column_tiers(column_edges, levels, columns):
    column_index = jnp.arange(columns)
    result = jnp.full((columns,), levels[-1], jnp.float32)
    for position in range(len(column_edges) - 1, -1, -1):
        result = jnp.where(column_index < column_edges[position], levels[position], result)
    return result


def signed_uniform(key, shape, distributed_copy):
    return jax.random.uniform(key, shape, jnp.float32, -1.0, 1.0) * 3.0 ** 0.5 * distributed_copy


def positive_square(key, shape, gradient):
    factor = jnp.exp(jax.random.uniform(key, shape, jnp.float32, 0.0, 1.3863))
    return factor * (0.001 / 0.999) * gradient * gradient


def mixer_gradient():
    return column_tiers([(QUERY_HEADS + 2 * KEY_VALUE_HEADS) * HEAD_SIZE], [0.4, 0.1], MIXER_COLUMNS) * TOKEN_COUNT ** 0.5


def dense_gradient():
    return column_tiers([2 * FF], [0.3, 0.5], DENSE_COLS) * TOKEN_COUNT ** 0.5


def gains_gradient():
    return column_tiers([2 * MODEL_WIDTH], [0.7, 0.4 * QUERY_HEADS ** 0.5], GAINS) * TOKEN_COUNT ** 0.5


def draw_seq_lengths(key, part):
    key = jax.random.fold_in(key, 11)
    first_key, second_key, third_key = jax.random.split(key, 3)
    unit_rows = NSHIFT * TOK_DEV // 16
    paired = (SEQS - 4) // 2
    middle_extra = jax.random.randint(first_key, (1,), 0, 4 * unit_rows + 1)
    special = jnp.concatenate([jnp.array([12 * unit_rows], jnp.int32), middle_extra.astype(jnp.int32), (4 * unit_rows - middle_extra).astype(jnp.int32), jnp.zeros((1,), jnp.int32)])
    random_extra = jax.random.randint(second_key, (paired,), 0, 8 * unit_rows + 1).astype(jnp.int32)
    extras = jnp.concatenate([special, random_extra, 8 * unit_rows - random_extra])
    order = jax.random.permutation(third_key, SEQS)
    return (SHORTEST_LENGTH + extras[order]).astype(jnp.int32)


def draw_mixer_master(key, part):
    key = jax.random.fold_in(key, 1)
    distributed_copy = column_tiers([(QUERY_HEADS + 2 * KEY_VALUE_HEADS) * HEAD_SIZE], [MODEL_WIDTH ** (-0.5), (QUERY_HEADS * HEAD_SIZE * 64 // SHORTEST_LENGTH) ** (-0.5)], MIXER_COLUMNS)
    return signed_uniform(key, (MODEL_WIDTH, MIXER_COLUMNS), distributed_copy[None, :])


def draw_mixer_moment(key, part):
    key = jax.random.fold_in(key, 2)
    return signed_uniform(key, (MODEL_WIDTH, MIXER_COLUMNS), 0.111 * mixer_gradient()[None, :])


def draw_mixer_square(key, part):
    key = jax.random.fold_in(key, 3)
    return positive_square(key, (MODEL_WIDTH, MIXER_COLUMNS), mixer_gradient()[None, :])


def draw_dense_master(key, part):
    key = jax.random.fold_in(key, 4)
    distributed_copy = column_tiers([2 * FF], [MODEL_WIDTH ** (-0.5), FF ** (-0.5)], DENSE_COLS)
    return signed_uniform(key, (MODEL_WIDTH, DENSE_COLS), distributed_copy[None, :])


def draw_dense_moment(key, part):
    key = jax.random.fold_in(key, 5)
    return signed_uniform(key, (MODEL_WIDTH, DENSE_COLS), 0.111 * dense_gradient()[None, :])


def draw_dense_square(key, part):
    key = jax.random.fold_in(key, 6)
    return positive_square(key, (MODEL_WIDTH, DENSE_COLS), dense_gradient()[None, :])


def draw_gains_master(key, part):
    key = jax.random.fold_in(key, 7)
    return jax.random.uniform(key, (GAINS,), jnp.float32, 0.6, 1.4)


def draw_gains_moment(key, part):
    key = jax.random.fold_in(key, 8)
    return signed_uniform(key, (GAINS,), 0.111 * gains_gradient())


def draw_gains_square(key, part):
    key = jax.random.fold_in(key, 9)
    return positive_square(key, (GAINS,), gains_gradient())


def block_scale(key, dims, pieces, smallest, top_value):
    def one(dim, parts):
        steps = jax.random.uniform(jax.random.fold_in(jax.random.fold_in(key, 6), dim), (parts,), jnp.float32, smallest / len(pieces), top_value / len(pieces))
        return jnp.repeat(jnp.exp(steps), dims[dim] // parts).reshape((-1,) + (1,) * (len(dims) - dim - 1))

    gain = one(*pieces[0])
    for cut in pieces[1:]:
        gain = gain * one(*cut)
    return gain


def gaussian(rng, extent, width, limit, shards=(), kind=jnp.bfloat16):
    level = block_scale(rng, extent, shards, -0.22, 0.18) if shards else 1.0
    values = jax.random.normal(rng, extent, jnp.float32) * width * level
    return jnp.minimum(jnp.maximum(values, -limit), limit).astype(kind)


def setup_inputs(seed: int = 0) -> dict:
    keys = jax.random.split(jax.random.key(seed), 13)
    return {
        "residual_in": gaussian(keys[0], (TOKEN_COUNT, MODEL_WIDTH), 1.0, 6.0, ((0, 32),)),
        "cotangent": gaussian(keys[1], (TOKEN_COUNT, MODEL_WIDTH), 1.0, 6.0, ((0, 32),)),
        "seq_lengths": draw_seq_lengths(jax.random.fold_in(keys[12], 71), 0),
        "mixer_master": draw_mixer_master(jax.random.fold_in(keys[12], 71), 0),
        "mixer_moment": draw_mixer_moment(jax.random.fold_in(keys[12], 71), 0),
        "mixer_square": draw_mixer_square(jax.random.fold_in(keys[12], 71), 0),
        "dense_master": draw_dense_master(jax.random.fold_in(keys[12], 71), 0),
        "dense_moment": draw_dense_moment(jax.random.fold_in(keys[12], 71), 0),
        "dense_square": draw_dense_square(jax.random.fold_in(keys[12], 71), 0),
        "gains_master": draw_gains_master(jax.random.fold_in(keys[12], 71), 0),
        "gains_moment": draw_gains_moment(jax.random.fold_in(keys[12], 71), 0),
        "gains_square": draw_gains_square(jax.random.fold_in(keys[12], 71), 0),
    }


@jax.custom_vjp
def reduced_copy(v):
    return lax.optimization_barrier(v.astype(jnp.bfloat16)).astype(jnp.float32)

@jax.custom_vjp
def low_back(v):
    return v

def low_keep(v):
    return (reduced_copy(v), None)

def low_pass(kept, grad):
    return (grad,)

def back_keep(v):
    return (v, None)

def back_low(kept, grad):
    return (reduced_copy(grad),)
reduced_copy.defvjp(low_keep, low_pass)
low_back.defvjp(back_keep, back_low)
norm_eps = 1e-06
rope_base = 1000000.0
masked_score = -1e+30
beta_first = 0.9
beta_second = 0.999
adam_eps = 1e-08
rate_matrix = 0.05
rate_gains = 0.5
decay_weight = 0.1

def highest(left_side, right_side):
    return jnp.dot(left_side, right_side, precision=lax.Precision.HIGHEST, preferred_element_type=jnp.float32)

def highest_last(left_side, right_side):
    return lax.dot_general(left_side, right_side, (((1,), (1,)), ((), ())), precision=lax.Precision.HIGHEST, preferred_element_type=jnp.float32)

def rms_scale(v, gain_row):
    return v * lax.rsqrt(lax.optimization_barrier(jnp.mean(v * v, axis=-1, keepdims=True)) + norm_eps) * gain_row

def rotate(v, token_positions):
    half_dim = v.shape[-1] // 2
    inverse = rope_base ** (-jnp.arange(half_dim, dtype=jnp.float32) * 2.0 / v.shape[-1])
    angles = token_positions.astype(jnp.float32)[:, None] * inverse[None, :]
    cosine = jnp.cos(angles)[:, None, :]
    sine_part = jnp.sin(angles)[:, None, :]
    lower_half = v[..., :half_dim]
    upper_half = v[..., half_dim:]
    return jnp.concatenate([lower_half * cosine - upper_half * sine_part, upper_half * cosine + lower_half * sine_part], axis=-1)

def head_prepared(raw_heads, gain_row, token_positions):
    return rotate(rms_scale(raw_heads, gain_row), token_positions)

def segment_of(seq_lengths, tokens):
    seq_ends = jnp.cumsum(seq_lengths).astype(jnp.int32)
    passed = (seq_ends[None, :] <= tokens[:, None]).astype(jnp.int32)
    segment = lax.optimization_barrier(jnp.sum(passed, axis=1)).astype(jnp.int32)
    token_positions = (tokens - lax.optimization_barrier(jnp.sum(passed * seq_lengths[None, :], axis=1))).astype(jnp.int32)
    return (segment, token_positions)

def attention(query_rows, key_row_block, value_rows, tokens, segment):
    query_block = min(512, TOKEN_COUNT)
    window = min(MAX_LEN + query_block, TOKEN_COUNT)
    query_group_width = QUERY_HEADS // KEY_VALUE_HEADS
    score_scale = HEAD_SIZE ** (-0.5)

    def block_fn(leading_row):
        key_first = jnp.clip(leading_row + query_block - window, 0, TOKEN_COUNT - window).astype(jnp.int32)
        query_block_rows = lax.dynamic_slice_in_dim(query_rows, leading_row, query_block, 0).reshape(query_block, KEY_VALUE_HEADS, query_group_width, HEAD_SIZE)
        block_k = lax.dynamic_slice_in_dim(key_row_block, key_first, window, 0)
        block_v = lax.dynamic_slice_in_dim(value_rows, key_first, window, 0)
        query_tokens = lax.dynamic_slice_in_dim(tokens, leading_row, query_block, 0)
        query_segment = lax.dynamic_slice_in_dim(segment, leading_row, query_block, 0)
        key_tokens = lax.dynamic_slice_in_dim(tokens, key_first, window, 0)
        key_segment = lax.dynamic_slice_in_dim(segment, key_first, window, 0)
        scores = jnp.einsum('qkgd,skd->kgqs', query_block_rows, block_k, precision=lax.Precision.HIGHEST, preferred_element_type=jnp.float32) * score_scale
        scores = low_back(scores)
        allowed = (query_segment[:, None] == key_segment[None, :]) & (key_tokens[None, :] <= query_tokens[:, None])
        scores = jnp.where(allowed[None, None], scores, masked_score)
        row_top = lax.optimization_barrier(jnp.max(scores, axis=-1, keepdims=True))
        exponent = jnp.exp(scores - row_top)
        probable = exponent / lax.optimization_barrier(jnp.sum(exponent, axis=-1, keepdims=True))
        head_output = jnp.einsum('kgqs,skd->qkgd', reduced_copy(probable), block_v, precision=lax.Precision.HIGHEST, preferred_element_type=jnp.float32)
        return head_output.reshape(query_block, QUERY_HEADS * HEAD_SIZE)
    starts = jnp.arange(TOKEN_COUNT // query_block, dtype=jnp.int32) * query_block
    return lax.map(jax.checkpoint(block_fn), starts).reshape(TOKEN_COUNT, QUERY_HEADS * HEAD_SIZE)

def adamw_update(weights, moment, square, gradient, step_rate, decay_rate):
    moment_new = beta_first * moment + (1.0 - beta_first) * gradient
    square_new = beta_second * square + (1.0 - beta_second) * gradient * gradient
    corrected = moment_new / (1.0 - beta_first ** STEP) / (jnp.sqrt(square_new / (1.0 - beta_second ** STEP)) + adam_eps)
    return (weights - step_rate * (corrected + decay_rate * weights), moment_new, square_new)

def reference(residual_in, cotangent, seq_lengths, mixer_master, mixer_moment, mixer_square, dense_master, dense_moment, dense_square, gains_master, gains_moment, gains_square):
    tokens = jnp.arange(TOKEN_COUNT, dtype=jnp.int32)
    segment, token_positions = segment_of(seq_lengths, tokens)
    query_key_value_columns = (QUERY_HEADS + 2 * KEY_VALUE_HEADS) * HEAD_SIZE

    def forward(residual, mixer_low, dense_low, gain_vector):
        mixer_gain = gain_vector[:MODEL_WIDTH]
        dense_gain = gain_vector[MODEL_WIDTH:2 * MODEL_WIDTH]
        query_gain = gain_vector[2 * MODEL_WIDTH:2 * MODEL_WIDTH + HEAD_SIZE]
        key_norm_gain = gain_vector[2 * MODEL_WIDTH + HEAD_SIZE:]
        normed = reduced_copy(rms_scale(residual, mixer_gain))
        projected_output = low_back(highest(normed, mixer_low[:, :query_key_value_columns]))
        query_rows = reduced_copy(head_prepared(projected_output[:, :QUERY_HEADS * HEAD_SIZE].reshape(TOKEN_COUNT, QUERY_HEADS, HEAD_SIZE), query_gain, token_positions))
        key_row_block = reduced_copy(head_prepared(projected_output[:, QUERY_HEADS * HEAD_SIZE:(QUERY_HEADS + KEY_VALUE_HEADS) * HEAD_SIZE].reshape(TOKEN_COUNT, KEY_VALUE_HEADS, HEAD_SIZE), key_norm_gain, token_positions))
        value_rows = reduced_copy(projected_output[:, (QUERY_HEADS + KEY_VALUE_HEADS) * HEAD_SIZE:].reshape(TOKEN_COUNT, KEY_VALUE_HEADS, HEAD_SIZE))
        attended = reduced_copy(low_back(attention(query_rows, key_row_block, value_rows, tokens, segment)))
        middle = residual + low_back(highest_last(attended, mixer_low[:, query_key_value_columns:]))
        normed_two = reduced_copy(rms_scale(middle, dense_gain))
        gate_up = low_back(highest(normed_two, dense_low[:, :2 * FF]))
        hidden = reduced_copy(jax.nn.silu(gate_up[:, :FF]) * gate_up[:, FF:])
        return middle + highest_last(hidden, dense_low[:, 2 * FF:])
    output, pullback = jax.vjp(forward, residual_in.astype(jnp.float32), reduced_copy(mixer_master), reduced_copy(dense_master), reduced_copy(gains_master))
    residual_grad, mixer_grad, dense_grad, gains_grad = pullback(cotangent.astype(jnp.float32))
    mixer_renewed, mixer_momentum, mixer_variance = adamw_update(mixer_master, mixer_moment, mixer_square, mixer_grad, rate_matrix, decay_weight)
    dense_renewed, dense_momentum, dense_variance = adamw_update(dense_master, dense_moment, dense_square, dense_grad, rate_matrix, decay_weight)
    gains_renewed, gains_momentum, gains_variance = adamw_update(gains_master, gains_moment, gains_square, gains_grad, rate_gains, 0.0)
    return (output.astype(jnp.bfloat16), residual_grad, mixer_renewed, mixer_momentum, mixer_variance, dense_renewed, dense_momentum, dense_variance, gains_renewed, gains_momentum, gains_variance)
```

```python
import functools

import jax
import jax.numpy as jnp
from jax import lax
from jax.experimental import pallas as pl
from jax.experimental.pallas import tpu as pltpu
from jax.sharding import PartitionSpec as P

MODEL_WIDTH = 1024
QUERY_HEADS = 16
KEY_VALUE_HEADS = 8
HEAD_SIZE = 128
FF = 3072
NSHIFT = 8
STEP = 10


norm_eps = 1e-06
rope_base = 1000000.0
masked_score = -1e30
beta_first = 0.9
beta_second = 0.999
adam_eps = 1e-08
rate_matrix = 0.05
rate_gains = 0.5
decay_weight = 0.1
log2_e = 1.4426950408889634
vmem_bytes = 56 * 1024 * 1024
MESH = pl.DeviceIdType.MESH
SLOTS = NSHIFT + 2
HOPS = NSHIFT // 2


def contract_first(left_side, right_side):
    return lax.dot_general(
        left_side, right_side, (((0,), (0,)), ((), ())), preferred_element_type=jnp.float32
    )


def contract_last(left_side, right_side):
    return lax.dot_general(
        left_side, right_side, (((1,), (1,)), ((), ())), preferred_element_type=jnp.float32
    )


def rms_scale(v, gain_row):
    return v * lax.rsqrt(jnp.mean(v * v, axis=-1, keepdims=True) + norm_eps) * gain_row


def rotate(v, token_positions):
    half_dim = v.shape[-1] // 2
    inverse = rope_base ** (-jnp.arange(half_dim, dtype=jnp.float32) * 2.0 / v.shape[-1])
    angles = token_positions.astype(jnp.float32)[:, None] * inverse[None, :]
    cosine = jnp.cos(angles)[:, None, :]
    sine_part = jnp.sin(angles)[:, None, :]
    lower_half = v[..., :half_dim]
    upper_half = v[..., half_dim:]
    return jnp.concatenate(
        [
            lower_half * cosine - upper_half * sine_part,
            upper_half * cosine + lower_half * sine_part,
        ],
        axis=-1,
    )


def segment_of(seq_lengths, tokens):
    seq_ends = jnp.cumsum(seq_lengths)
    passed = (seq_ends[None, :] <= tokens[:, None]).astype(jnp.int32)
    segment = jnp.sum(passed, axis=1)
    token_positions = tokens - jnp.sum(passed * seq_lengths[None, :], axis=1)
    return (segment, token_positions)


def swiglu(gate_pre, up_act):
    return jax.nn.silu(gate_pre) * up_act


def adamw_update(weights, moment, square, gradient, step_rate, decay_rate):
    moment_new = beta_first * moment + (1.0 - beta_first) * gradient
    square_new = beta_second * square + (1.0 - beta_second) * gradient * gradient
    corrected = (
        moment_new
        / (1.0 - beta_first**STEP)
        / (jnp.sqrt(square_new / (1.0 - beta_second**STEP)) + adam_eps)
    )
    return (weights - step_rate * (corrected + decay_rate * weights), moment_new, square_new)


def place_of(me):
    chip = me // 2
    return chip // 4, chip % 4, me % 2


def device_at(plane, spot, core):
    return (plane * 4 + spot) * 2 + core


def across(spot, bit):
    over_x = spot + 1 - 2 * (spot % 2)
    if bit == 1:
        return over_x
    start = spot if bit == 2 else over_x
    return start + 2 - 4 * (start // 2)


def first_and_second(spot, core):
    over_x, over_y = across(spot, 1), across(spot, 2)
    return over_x + (over_y - over_x) * core, over_y + (over_x - over_y) * core


def greet(devices):
    barrier = pltpu.get_barrier_semaphore()
    for device in devices:
        pl.semaphore_signal(barrier, inc=1, device_id=(device,), device_id_type=MESH)
    pl.semaphore_wait(barrier, len(devices))


def remote(source, target, send_sem, recv_sem, device):
    return pltpu.make_async_remote_copy(
        src_ref=source,
        dst_ref=target,
        send_sem=send_sem,
        recv_sem=recv_sem,
        device_id=(device,),
        device_id_type=MESH,
    )


def gather_kernel(planes, block_ref, all_ref, own_sem, z_send, z_recv, a_send, a_recv, b_send, b_recv, c_send, c_recv):
    me = lax.axis_index("dp")
    plane, spot, core = place_of(me)
    near, far = first_and_second(spot, core)
    diagonal = across(spot, 3)
    sibling = device_at(plane, spot, 1 - core)
    near_device, far_device = device_at(plane, near, core), device_at(plane, far, core)
    others = [device_at((plane + step) % planes, spot, core) for step in range(1, planes)]
    greet([sibling, near_device, far_device] + others)
    started = []

    def send(block, source, send_sem, recv_sem, device):
        copy = remote(source, all_ref.at[block], send_sem, recv_sem, device)
        copy.start()
        started.append(copy)

    def arrived(block, recv_sem):
        remote(block_ref, all_ref.at[block], own_sem, recv_sem, sibling).wait_recv()

    for step in range(1, planes):
        send(me, block_ref, z_send.at[step - 1], z_recv.at[step - 1], others[step - 1])
    send(me, block_ref, a_send.at[0], a_recv.at[0], near_device)
    send(me, block_ref, b_send.at[0], b_recv.at[0], far_device)
    send(me, block_ref, c_send.at[0], c_recv.at[0], sibling)
    own = pltpu.make_async_copy(block_ref, all_ref.at[me], own_sem)
    own.start()
    for step in range(planes):
        from_plane = (plane - step + planes) % planes
        if step:
            block = device_at(from_plane, spot, core)
            arrived(block, z_recv.at[step - 1])
            send(block, all_ref.at[block], a_send.at[step], a_recv.at[step], near_device)
            send(block, all_ref.at[block], b_send.at[step], b_recv.at[step], far_device)
            send(block, all_ref.at[block], c_send.at[step], c_recv.at[step], sibling)
        block = device_at(from_plane, near, core)
        slot = planes + step
        arrived(block, a_recv.at[step])
        send(block, all_ref.at[block], b_send.at[slot], b_recv.at[slot], far_device)
        send(block, all_ref.at[block], c_send.at[slot], c_recv.at[slot], sibling)
    for index in range(2 * planes):
        step = index % planes
        from_plane = (plane - step + planes) % planes
        block = device_at(from_plane, far if index < planes else diagonal, core)
        slot = 2 * planes + index
        arrived(block, b_recv.at[index])
        send(block, all_ref.at[block], c_send.at[slot], c_recv.at[slot], sibling)
    own.wait()
    near, far = first_and_second(spot, 1 - core)
    for index in range(4 * planes):
        group, step = index // planes, index % planes
        from_plane = (plane - step + planes) % planes
        block = device_at(from_plane, (spot, near, far, diagonal)[group], 1 - core)
        arrived(block, c_recv.at[index])
    for copy in started:
        copy.wait_send()


def gather_blocks(block, devices):
    planes = devices // 8
    sems = pltpu.SemaphoreType.DMA
    return pl.pallas_call(
        functools.partial(gather_kernel, planes),
        out_shape=jax.ShapeDtypeStruct((devices,) + block.shape, block.dtype),
        in_specs=[pl.BlockSpec(memory_space=pl.ANY)],
        out_specs=pl.BlockSpec(memory_space=pl.ANY),
        scratch_shapes=[sems]
        + [sems((max(planes - 1, 1),))] * 2
        + [sems((planes,))] * 2
        + [sems((2 * planes,))] * 2
        + [sems((4 * planes,))] * 2,
        compiler_params=pltpu.CompilerParams(
            collective_id=0, has_side_effects=True, vmem_limit_bytes=vmem_bytes
        ),
        name="gather_weights",
    )(block)


KV_PARTS = 4


def spread_kernel(
    planes, own_ref, held_ref, zero_ref, zero_sem, own_sem, z_send, z_recv, p_send, p_recv, c_send, c_recv
):
    me = lax.axis_index("dp")
    plane, spot, core = place_of(me)
    sibling = device_at(plane, spot, 1 - core)
    after, before = (plane + 1) % planes, (plane - 1 + planes) % planes
    spots = [across(spot, bit) for bit in (1, 2, 3)]
    mates = [device_at(plane, there, core) for there in spots]
    after_device, before_device = device_at(after, spot, core), device_at(before, spot, core)
    greet([sibling, after_device, before_device] + mates if planes > 1 else [sibling] + mates)
    has_before, has_after = plane > 0, plane < planes - 1
    rows = own_ref.shape[1] // KV_PARTS
    parts = [pl.ds(part * rows, rows) for part in range(KV_PARTS)]
    mine = 1 - core

    def piece(ref, part):
        return ref.at[pl.ds(2, 2), parts[part]]

    def held(hops, part):
        return held_ref.at[2 * hops + mine, :, parts[part]]

    own_copies = []
    for part in range(KV_PARTS):
        copy = pltpu.make_async_copy(piece(own_ref, part), held(0, part), own_sem.at[part])
        copy.start()
        own_copies.append(copy)

    def z_copy(part):
        return remote(piece(own_ref, part), held(HOPS, part), z_send.at[part], z_recv.at[part], after_device)

    def mate_copy(index, part, later):
        there = spots[index]
        source = piece(own_ref, part) if later else held(HOPS, part)
        hops = there - spot if later else there + 4 - spot
        return remote(source, held(hops, part), p_send.at[index, part], p_recv.at[index, part], mates[index])

    def core_copy(hops, part):
        source = piece(own_ref, part) if hops == 0 else held(hops, part)
        return remote(source, held(hops, part), c_send.at[hops, part], c_recv.at[hops, part], sibling)

    zero_ref[...] = jnp.zeros(zero_ref.shape, zero_ref.dtype)

    def zero_copy(slot):
        return pltpu.make_async_copy(zero_ref, held_ref.at[slot], zero_sem.at[slot])

    for hops in range(1, HOPS + 1):

        @pl.when((spot < hops) & (plane == 0))
        def _():
            zero_copy(2 * hops).start()
            zero_copy(2 * hops + 1).start()

    @pl.when(has_after)
    def _():
        for part in range(KV_PARTS):
            z_copy(part).start()

    for index in range(3):

        @pl.when(spots[index] > spot)
        def _():
            for part in range(KV_PARTS):
                mate_copy(index, part, True).start()

    for part in range(KV_PARTS):
        core_copy(0, part).start()

    for part in range(KV_PARTS):

        @pl.when(has_before)
        def _():
            z_copy(part).wait_recv()
            core_copy(HOPS, part).start()
            for index in range(3):

                @pl.when(spots[index] < spot)
                def _():
                    mate_copy(index, part, False).start()

    for part in range(KV_PARTS):
        for index in range(3):
            there = spots[index]
            for hops in (1, 2, 3):
                @pl.when((spot - there == hops) | ((spot + 4 - there == hops) & has_before))
                def _():
                    remote(
                        piece(own_ref, part), held(hops, part), p_send.at[index, part],
                        p_recv.at[index, part], mates[index],
                    ).wait_recv()
                    core_copy(hops, part).start()

    for hops in range(1, HOPS + 1):

        @pl.when((spot < hops) & (plane == 0))
        def _():
            zero_copy(2 * hops).wait()
            zero_copy(2 * hops + 1).wait()

    for copy in own_copies:
        copy.wait()
    for part in range(KV_PARTS):
        core_copy(0, part).wait()
        for hops in range(1, HOPS + 1):

            @pl.when((spot - hops >= 0) | has_before)
            def _():
                core_copy(hops, part).wait()

        @pl.when(has_after)
        def _():
            z_copy(part).wait_send()

        for index in range(3):

            @pl.when(spots[index] > spot)
            def _():
                mate_copy(index, part, True).wait_send()

            @pl.when((spots[index] < spot) & has_before)
            def _():
                mate_copy(index, part, False).wait_send()


def spread_keys(own, devices):
    planes = devices // 8
    sems = pltpu.SemaphoreType.DMA
    return pl.pallas_call(
        functools.partial(spread_kernel, planes),
        out_shape=jax.ShapeDtypeStruct((SLOTS, 2) + own.shape[1:], own.dtype),
        in_specs=[pl.BlockSpec(memory_space=pl.ANY)],
        out_specs=pl.BlockSpec(memory_space=pl.ANY),
        scratch_shapes=[
            pltpu.VMEM((2,) + own.shape[1:], own.dtype),
            sems((SLOTS,)),
            sems((KV_PARTS,)),
            sems((KV_PARTS,)),
            sems((KV_PARTS,)),
            sems((3, KV_PARTS)),
            sems((3, KV_PARTS)),
            sems((HOPS + 1, KV_PARTS)),
            sems((HOPS + 1, KV_PARTS)),
        ],
        compiler_params=pltpu.CompilerParams(
            collective_id=1, has_side_effects=True, vmem_limit_bytes=vmem_bytes
        ),
        name="spread_keys",
    )(own)


def swapped(v):
    return jnp.concatenate([v[:, HEAD_SIZE // 2 :], v[:, : HEAD_SIZE // 2]], axis=1)


def head_forward(raw, gain_row, cosine, sine):
    turned = rms_scale(raw, gain_row)
    return turned * cosine + swapped(turned) * sine


def norm_back(grad, v, gain_row):
    scale = lax.rsqrt(jnp.mean(v * v, axis=-1, keepdims=True) + norm_eps)
    weighed = grad * gain_row
    inner = jnp.mean(weighed * v, axis=-1, keepdims=True)
    v_grad = scale * weighed - v * (scale * scale * scale * inner)
    return v_grad, jnp.sum(grad * v * scale, axis=0, keepdims=True)


def head_back(grad, raw, gain_row, cosine, sine):
    return norm_back(grad * cosine + swapped(grad * sine), raw, gain_row)


def last_kernel(planes, *refs):
    (a_ref, b_first_ref, b_last_ref, kept_ref, arrived_ref, whole_ref, first_ref, last_ref, weight_ref, input_ref, gain_ref, middle_ref, gains_ref,
     out_ref, passed_out, whole_out, residual_ref, gains_out,
     a_all, right, grads, got_one, got_two, got_z, passing, swap_out, swap_in, kept_own, kept_got, got_far, passed, got_passed, passed_sum, passed_in,
     got_whole, whole_far, got_whole_far, whole_sum, whole_in, weights, back,
     gains_in, x_send, x_recv, own_sem, one_send, one_recv, two_send, two_recv, z_send, z_recv, s_send, s_recv,
     g_send, g_recv, f_send, f_recv, q_send, q_recv, h_send, h_recv, v_send, v_recv, load_sem) = refs
    me = lax.axis_index("dp")
    plane, spot, core = place_of(me)
    near, far = first_and_second(spot, core)
    diagonal = across(spot, 3)
    sibling = device_at(plane, spot, 1 - core)
    near_device, far_device = device_at(plane, near, core), device_at(plane, far, core)
    others = [device_at((plane - 1 - step + 2 * planes) % planes, spot, core) for step in range(planes - 1)]
    tokens = a_ref.shape[0]
    columns = b_first_ref.shape[1]
    chunks, blocks, block_rows = grads.shape[0], grads.shape[1], grads.shape[2]
    group = blocks // 4
    rows = out_ref.shape[0]
    partners = []
    bit = 1
    while bit < planes * 8:
        partners.append(me + bit - 2 * bit * ((me // bit) % 2))
        bit *= 2
    greet([sibling, near_device, far_device] + others)

    def gains_copy(step):
        return remote(gains_out, gains_in.at[step], g_send.at[step], g_recv.at[step], partners[step])

    def gains_step(step):
        if step > len(partners):
            return
        if step:
            gains_copy(step - 1).wait()
            gains_out[...] += gains_in[step - 1]
        if step < len(partners):
            gains_copy(step).start()

    theirs, ours = pl.ds(tokens, tokens), pl.ds(0, tokens)
    exchanges = [
        remote(a_ref, a_all.at[theirs], x_send.at[0], x_recv.at[0], sibling),
        remote(b_first_ref, right.at[theirs], x_send.at[1], x_recv.at[1], sibling),
    ]
    locals_ = [
        pltpu.make_async_copy(a_ref, a_all.at[ours], own_sem.at[0]),
        pltpu.make_async_copy(b_first_ref, right.at[ours], own_sem.at[1]),
    ]
    exchanges[0].start()
    locals_[0].start()

    @pl.when(core == 0)
    def _():
        remote(b_last_ref, right.at[theirs], x_send.at[1], x_recv.at[1], sibling).start()
        locals_[1].start()

    @pl.when(core == 1)
    def _():
        exchanges[1].start()
        pltpu.make_async_copy(b_last_ref, right.at[ours], own_sem.at[1]).start()

    targets = [(plane + 1 + step) % planes for step in range(planes)]

    def far_copy(step):
        return remote(
            kept_own.at[1, targets[step]], got_far.at[targets[step]], f_send.at[step], f_recv.at[step], far_device
        )

    def passed_copy(step):
        target = (plane - 1 - step + 2 * planes) % planes
        return remote(passed.at[target], got_passed.at[step], q_send.at[step], q_recv.at[step], others[step])

    def whole_copy(side):
        return remote(
            whole_ref.at[(near, diagonal)[side]], got_whole.at[side], h_send.at[side], h_recv.at[side], near_device
        )

    whole_far_copy = remote(whole_far, got_whole_far, v_send, v_recv, far_device)
    for side in (1, 0):
        whole_copy(side).start()
    kept_loads = [
        pltpu.make_async_copy(kept_ref, kept_own, own_sem.at[2]),
        pltpu.make_async_copy(arrived_ref, kept_got, own_sem.at[3]),
    ]
    for copy in kept_loads:
        copy.start()
    load = pltpu.make_async_copy(weight_ref.at[:, pl.ds(0, 2 * columns)], weights, load_sem)
    load.start()
    for copy in kept_loads:
        copy.wait()
    for step in range(planes):
        target = targets[step]
        both = kept_own[1, target].astype(jnp.float32) + kept_got[1, target].astype(jnp.float32)
        kept_own[1, target] = both.astype(jnp.bfloat16)
        far_copy(step).start()
    for copy in locals_:
        copy.wait()
    for copy in exchanges:
        copy.wait_recv()

    order = [(plane // group + 1 + step) % chunks for step in range(chunks)]
    width = 512
    chunk_rows = blocks * block_rows

    def multiply(chunk):
        strip = a_all[:, pl.ds(pl.multiple_of(chunk * chunk_rows, 128), chunk_rows)].T

        def one(index, carry):
            cut = pl.ds(pl.multiple_of(index * width, 128), width)
            product = jnp.dot(strip, right[:, cut], preferred_element_type=jnp.float32)
            grads[chunk, :, :, cut] = product.astype(jnp.bfloat16).reshape(blocks, block_rows, width)
            return carry

        lax.fori_loop(0, columns // width, one, 0)

    def one_copy(index, member, side):
        chunk = order[index]
        spot_there = (near, diagonal)[side]
        return remote(
            grads.at[chunk, member * 4 + spot_there], got_one.at[index, member, side],
            one_send.at[index, member, side], one_recv.at[index, member, side], near_device,
        )

    def two_copy(index, member):
        return remote(
            grads.at[order[index], member * 4 + far], got_two.at[index, member],
            two_send.at[index, member], two_recv.at[index, member], far_device,
        )

    def z_copy(index, member, step):
        return remote(
            passing.at[index, member], got_z.at[step], z_send.at[step], z_recv.at[step], others[step]
        )

    def add_one(index):
        chunk = order[index]
        for member in range(group):
            for side in (1, 0):
                one_copy(index, member, side).wait_recv()
                block = member * 4 + (spot, far)[side]
                both = grads[chunk, block].astype(jnp.float32) + got_one[index, member, side].astype(jnp.float32)
                grads[chunk, block] = both.astype(jnp.bfloat16)
                if side:
                    two_copy(index, member).start()

    def add_two(index):
        chunk = order[index]
        for member in range(group):
            two_copy(index, member).wait_recv()
            both = grads[chunk, member * 4 + spot].astype(jnp.float32) + got_two[index, member].astype(jnp.float32)
            to_plane = chunk * group + member
            passing[index, member] = both.astype(jnp.bfloat16)
            for step in range(planes - 1):

                @pl.when((plane - 1 - step + 2 * planes) % planes == to_plane)
                def _():
                    z_copy(index, member, step).start()

            if index == chunks - 1:

                @pl.when(to_plane == plane)
                def _():
                    swap_out[...] = both

    def add_far(step):
        target = targets[step]
        far_copy(step).wait_recv()
        both = kept_own[0, target].astype(jnp.float32) + kept_got[0, target].astype(jnp.float32)
        both += got_far[target].astype(jnp.float32)
        if step == planes - 1:
            passed_sum[...] = both
        else:
            passed[target] = both.astype(jnp.bfloat16)
            passed_copy(planes - 2 - step).start()

    def input_gradient():
        load.wait()
        back[...] = contract_last(first_ref[...], weights[:, :columns])
        total = back[...] + contract_last(last_ref[...], weights[:, columns:])
        part, gain_grad = norm_back(total, input_ref[...].astype(jnp.float32), gain_ref[...])
        residual_ref[...] = middle_ref[...] + part
        gains_out[...] = gains_ref[...]
        for row in range(gain_grad.shape[1] // HEAD_SIZE):
            gains_out[row : row + 1] = gain_grad[:, row * HEAD_SIZE : (row + 1) * HEAD_SIZE]

    for index in range(chunks):
        multiply(order[index])
        for member in range(group):
            for side in (1, 0):
                one_copy(index, member, side).start()
        if index == 0:
            whole_copy(1).wait_recv()
            both = whole_ref[far].astype(jnp.float32) + got_whole[1].astype(jnp.float32)
            whole_far[...] = both.astype(jnp.bfloat16)
            whole_far_copy.start()
        if index == 0:
            for step in range(planes // 4):
                add_far(step)
        if index == min(1, chunks - 1):
            for step in range(planes // 4, planes // 2):
                add_far(step)
            input_gradient()
            for step in range(planes // 2, planes):
                add_far(step)
            gains_step(0)
        if index:
            add_one(index - 1)
        if index > 1:
            gains_step(index - 1)
        if index > 1:
            add_two(index - 2)
    turns_done = max(chunks - 1, 1)
    add_one(chunks - 1)
    gains_step(turns_done)
    if chunks > 1:
        add_two(chunks - 2)
    gains_step(turns_done + 1)
    add_two(chunks - 1)
    gains_step(turns_done + 2)
    for step in range(planes - 1):
        passed_copy(step).wait_recv()
        passed_sum[...] += got_passed[step].astype(jnp.float32)
    for step in range(planes - 1):
        z_copy(0, 0, step).wait_recv()
        swap_out[...] += got_z[step].astype(jnp.float32)
    whole_copy(0).wait_recv()
    whole_far_copy.wait_recv()
    whole_sum[...] = (
        whole_ref[spot].astype(jnp.float32) + got_whole[0].astype(jnp.float32) + got_whole_far[...].astype(jnp.float32)
    )
    mine = pl.ds(pl.multiple_of(core * rows, 8), rows)
    other = pl.ds(pl.multiple_of((1 - core) * rows, 8), rows)
    swaps = [
        remote(swap_out.at[other], swap_in, s_send.at[0], s_recv.at[0], sibling),
        remote(passed_sum.at[other], passed_in, s_send.at[1], s_recv.at[1], sibling),
        remote(whole_sum.at[other], whole_in, s_send.at[2], s_recv.at[2], sibling),
    ]
    for swap in swaps:
        swap.start()
    out_ref[:, pl.ds(pl.multiple_of(core * columns, 128), columns)] = swap_out[mine, :]
    passed_out[core] = passed_sum[mine, :]
    whole_out[core] = whole_sum[mine, :]
    for step in range(turns_done + 3, len(partners) + 1):
        gains_step(step)
    swaps[0].wait_recv()
    out_ref[:, pl.ds(pl.multiple_of((1 - core) * columns, 128), columns)] = swap_in[...]
    swaps[1].wait_recv()
    passed_out[1 - core] = passed_in[...]
    swaps[2].wait_recv()
    whole_out[1 - core] = whole_in[...]
    whole_far_copy.wait_send()
    for side in range(2):
        whole_copy(side).wait_send()
    for copy in exchanges + swaps:
        copy.wait_send()
    for index in range(chunks):
        for member in range(group):
            two_copy(index, member).wait_send()
            for side in (0, 1):
                one_copy(index, member, side).wait_send()
    for step in range(planes - 1):
        z_copy(0, 0, step).wait_send()
        passed_copy(step).wait_send()
    for step in range(planes):
        far_copy(step).wait_send()


def last_gradients(a, b_first, b_last, kept, arrived, whole, mixer_low, residual_in, mixer_gain, grad_middle, gains, devices, identity):
    planes = devices // 8
    tokens, width = a.shape
    rows = width // devices
    chunks = min(planes, 4)
    group = planes // chunks
    columns = b_first.shape[1]
    kept_columns = kept.shape[3]
    kept_block = (2 * rows, kept_columns)
    whole_block_shape = whole.shape[1:]
    turns = (devices - 1).bit_length()
    sems = pltpu.SemaphoreType.DMA
    low = jnp.bfloat16
    block = (2 * rows, columns)
    in_vmem = pl.BlockSpec(memory_space=pltpu.VMEM)
    in_any = pl.BlockSpec(memory_space=pl.ANY)
    others = max(planes - 1, 1)
    return pl.pallas_call(
        functools.partial(last_kernel, planes),
        out_shape=[
            jax.ShapeDtypeStruct((rows, 2 * columns), jnp.float32),
            jax.ShapeDtypeStruct((2, rows, kept_columns), jnp.float32),
            jax.ShapeDtypeStruct((2, rows, whole_block_shape[1]), jnp.float32),
            jax.ShapeDtypeStruct((tokens, width), jnp.float32),
            jax.ShapeDtypeStruct(gains.shape, jnp.float32),
        ],
        in_specs=[in_any] * 5 + [in_vmem] * 3 + [in_any] + [in_vmem] * 4,
        out_specs=[in_vmem] * 5,
        scratch_shapes=[
            pltpu.VMEM((2 * tokens, width), low),
            pltpu.VMEM((2 * tokens, columns), low),
            pltpu.VMEM((chunks, group * 4) + block, low),
            pltpu.VMEM((chunks, group, 2) + block, low),
            pltpu.VMEM((chunks, group) + block, low),
            pltpu.VMEM((others,) + block, low),
            pltpu.VMEM((chunks, group) + block, low),
            pltpu.VMEM(block, jnp.float32),
            pltpu.VMEM((rows, columns), jnp.float32),
            pltpu.VMEM((2, planes) + kept_block, low),
            pltpu.VMEM((2, planes) + kept_block, low),
            pltpu.VMEM((planes,) + kept_block, low),
            pltpu.VMEM((planes,) + kept_block, low),
            pltpu.VMEM((others,) + kept_block, low),
            pltpu.VMEM(kept_block, jnp.float32),
            pltpu.VMEM((rows, kept_columns), jnp.float32),
            pltpu.VMEM((2,) + whole_block_shape, low),
            pltpu.VMEM(whole_block_shape, low),
            pltpu.VMEM(whole_block_shape, low),
            pltpu.VMEM(whole_block_shape, jnp.float32),
            pltpu.VMEM((rows, whole_block_shape[1]), jnp.float32),
            pltpu.VMEM((width, 2 * columns), low),
            pltpu.VMEM((tokens, width), jnp.float32),
            pltpu.VMEM((turns,) + gains.shape, jnp.float32),
            sems((2,)),
            sems((2,)),
            sems((4,)),
            sems((chunks, group, 2)),
            sems((chunks, group, 2)),
            sems((chunks, group)),
            sems((chunks, group)),
            sems((others,)),
            sems((others,)),
            sems((3,)),
            sems((3,)),
            sems((turns,)),
            sems((turns,)),
            sems((planes,)),
            sems((planes,)),
            sems((others,)),
            sems((others,)),
            sems((2,)),
            sems((2,)),
            sems,
            sems,
            sems,
        ],
        compiler_params=pltpu.CompilerParams(
            collective_id=identity, has_side_effects=True, vmem_limit_bytes=vmem_bytes
        ),
        name="last_gradients",
    )(a, b_first, b_last, kept, arrived, whole, b_first, b_last, mixer_low, residual_in, mixer_gain, grad_middle, gains)


def routes(devices, target):
    return [(device, device_at(*target(*place_of(device)))) for device in range(devices)]


def to_near(block, devices):
    return lax.ppermute(
        block, "dp", routes(devices, lambda plane, spot, core: (plane, first_and_second(spot, core)[0], core))
    )


def over_slots(bounds_ref, one_slot):
    pairs, last = bounds_ref[1] // 2, bounds_ref[2]
    one_slot(0, 1, True)
    lax.fori_loop(0, pairs, lambda pair, carry: one_slot(2 * pair + 1, 2, False), None)
    lax.fori_loop(pairs, last // 2, lambda pair, carry: one_slot(2 * pair + 1, 2, True), None)
    lax.fori_loop(last // 2 * 2 + 1, last + 1, lambda slot, carry: one_slot(slot, 1, True), None)


def held_blocks(held_ref, slot, count, which):
    blocks = [held_ref[slot + index, which] for index in reversed(range(count))]
    return blocks[0] if count == 1 else jnp.concatenate(blocks, axis=0)


def allowed_keys(shape, key_axis, start, last_slot, tokens, own):
    place = lax.broadcasted_iota(jnp.int32, shape, key_axis) - last_slot * tokens
    allowed = place >= start
    if own is not None:
        allowed &= place <= own
    return allowed


def attend_kernel(
    bounds_ref, query_ref, held_ref, start_ref, row_start_ref, low_ref, high_ref, log_ref,
    stack_ref, sum_ref, value_ref, top_ref, weight_ref,
):
    groups = QUERY_HEADS // KEY_VALUE_HEADS
    tokens = query_ref.shape[0]
    scale = HEAD_SIZE ** (-0.5) * log2_e
    offset = bounds_ref[0]

    def bounded():
        value_ref[:, HEAD_SIZE:] = jnp.ones((2 * tokens, HEAD_SIZE), jnp.bfloat16)
        sum_ref[...] = jnp.zeros(sum_ref.shape, jnp.float32)

        def one_slot(slot, count, masked):
            keys = held_blocks(held_ref, offset + slot, count, 0)
            value_ref[: count * tokens, :HEAD_SIZE] = held_blocks(held_ref, offset + slot, count, 1)
            for group in range(groups):
                rows = slice(group * tokens, (group + 1) * tokens)
                query = query_ref[:, group * HEAD_SIZE : (group + 1) * HEAD_SIZE]
                weights = jnp.exp2(contract_last(query, keys) * scale)
                if masked:
                    own = lax.broadcasted_iota(jnp.int32, weights.shape, 0) if count == 1 else None
                    allowed = allowed_keys(weights.shape, 1, row_start_ref[...], slot + count - 1, tokens, own)
                    weights = jnp.where(allowed, weights, 0.0)
                sum_ref[rows] += jnp.dot(
                    weights.astype(jnp.bfloat16), value_ref[: count * tokens], preferred_element_type=jnp.float32
                )

        over_slots(bounds_ref, one_slot)
        for group in range(groups):
            rows = slice(group * tokens, (group + 1) * tokens)
            total = sum_ref[rows, HEAD_SIZE:]
            mixed = sum_ref[rows, :HEAD_SIZE] / total
            cut = slice(group * HEAD_SIZE, (group + 1) * HEAD_SIZE)
            low_ref[:, cut] = mixed.astype(jnp.bfloat16)
            high_ref[:, cut] = mixed
            log_ref[0, :, rows] = jnp.log2(total).T[:1]

    def running():
        top_ref[...] = jnp.full(top_ref.shape, masked_score, jnp.float32)
        weight_ref[...] = jnp.zeros(weight_ref.shape, jnp.float32)
        stack_ref[...] = jnp.zeros(stack_ref.shape, jnp.float32)

        def one_slot(slot, count, masked):
            keys = held_blocks(held_ref, offset + slot, count, 0)
            values = held_blocks(held_ref, offset + slot, count, 1)
            for group in range(groups):
                query = query_ref[:, group * HEAD_SIZE : (group + 1) * HEAD_SIZE]
                scores = contract_last(keys, query) * scale
                if masked:
                    own = lax.broadcasted_iota(jnp.int32, scores.shape, 1) if count == 1 else None
                    allowed = allowed_keys(scores.shape, 0, start_ref[:, :tokens], slot + count - 1, tokens, own)
                    scores = jnp.where(allowed, scores, masked_score)
                old = top_ref[group : group + 1]
                top = jnp.maximum(old, jnp.max(scores, axis=0, keepdims=True))
                weights = jnp.exp2(scores - top)
                shrink = jnp.exp2(old - top)
                top_ref[group : group + 1] = top
                weight_ref[group : group + 1] = weight_ref[group : group + 1] * shrink + jnp.sum(
                    weights, axis=0, keepdims=True
                )
                stack_ref[group] = stack_ref[group] * shrink + contract_first(values, weights.astype(jnp.bfloat16))

        over_slots(bounds_ref, one_slot)
        for group in range(groups):
            weight = weight_ref[group : group + 1]
            mixed = (stack_ref[group] / weight).T
            cut = slice(group * HEAD_SIZE, (group + 1) * HEAD_SIZE)
            low_ref[:, cut] = mixed.astype(jnp.bfloat16)
            high_ref[:, cut] = mixed
            log_ref[0, :, group * tokens : (group + 1) * tokens] = top_ref[group : group + 1] + jnp.log2(weight)

    pl.when(bounds_ref[3] > 0)(bounded)
    pl.when(bounds_ref[3] <= 0)(running)


def head_columns(tokens):
    wide = QUERY_HEADS // KEY_VALUE_HEADS * HEAD_SIZE
    per_block = KEY_VALUE_HEADS * HEAD_SIZE // wide
    return pl.BlockSpec((None, tokens, wide), lambda head, bounds: (head // per_block, 0, head % per_block))


def attend(bounds, prepared, held, start_row):
    tokens = prepared.shape[1]
    groups = QUERY_HEADS // KEY_VALUE_HEADS
    wide = groups * HEAD_SIZE
    by_head = pl.BlockSpec((tokens, wide), lambda head, bounds: (0, head))
    products = 4 * tokens * tokens * NSHIFT * HEAD_SIZE * QUERY_HEADS
    columns = QUERY_HEADS * HEAD_SIZE
    row_start = start_row[0, :tokens, None]

    def whole(array):
        return pl.BlockSpec(array.shape, lambda head, bounds: (0,) * array.ndim)

    return pl.pallas_call(
        attend_kernel,
        grid_spec=pltpu.PrefetchScalarGridSpec(
            num_scalar_prefetch=1,
            grid=(KEY_VALUE_HEADS,),
            in_specs=[
                head_columns(tokens),
                pl.BlockSpec((SLOTS, 2, tokens, HEAD_SIZE), lambda head, bounds: (0, 0, 0, head)),
                whole(start_row),
                whole(row_start),
            ],
            out_specs=[
                by_head,
                by_head,
                pl.BlockSpec((1, 1, groups * tokens), lambda head, bounds: (head, 0, 0)),
            ],
            scratch_shapes=[
                pltpu.VMEM((groups, HEAD_SIZE, tokens), jnp.float32),
                pltpu.VMEM((groups * tokens, 2 * HEAD_SIZE), jnp.float32),
                pltpu.VMEM((2 * tokens, 2 * HEAD_SIZE), jnp.bfloat16),
                pltpu.VMEM((groups, tokens), jnp.float32),
                pltpu.VMEM((groups, tokens), jnp.float32),
            ],
        ),
        out_shape=[
            jax.ShapeDtypeStruct((tokens, columns), jnp.bfloat16),
            jax.ShapeDtypeStruct((tokens, columns), jnp.float32),
            jax.ShapeDtypeStruct((KEY_VALUE_HEADS, 1, groups * tokens), jnp.float32),
        ],
        compiler_params=pltpu.CompilerParams(vmem_limit_bytes=vmem_bytes),
        cost_estimate=pl.CostEstimate(flops=products, bytes_accessed=20 * 2**20, transcendentals=0),
        name="attend",
    )(bounds, prepared, held, start_row, row_start)


def attend_back_kernel(
    planes, prepared_ref, held_ref, weight_ref, high_ref, raw_ref, kept_ref, arrived_ref, whole_ref,
    start_ref, branch_ref, log_ref, wave_ref, head_gain_ref,
    query_out, key_out, query_gain_ref, key_gain_ref, kept_out, whole_out,
    held_buf, query_buf, weight_buf, high_buf, raw_buf, raw_keys,
    sum_ref, stack_ref, grad_ref, delta_ref,
    mine, sending, theirs, in_plane, later, back, total,
    kept_own, kept_got, got_far, passed, got_passed, whole_own, got_whole, swap_out, swap_in,
    load_sem, keys_sem, c_send, c_recv, p_send, p_recv, z_send, z_recv, own_sem, f_send, f_recv, r_send, r_recv, v_send, v_recv, s_send, s_recv,
):
    heads, groups = KEY_VALUE_HEADS, QUERY_HEADS // KEY_VALUE_HEADS
    wide = groups * HEAD_SIZE
    tokens = branch_ref.shape[0]
    scale = HEAD_SIZE ** (-0.5)
    me = lax.axis_index("dp")
    plane, spot, core = place_of(me)
    sibling = device_at(plane, spot, 1 - core)
    before = (plane - 1 + planes) % planes
    spots = [across(spot, bit) for bit in (1, 2, 3)]
    mates = [device_at(plane, there, core) for there in spots]
    before_device = device_at(before, spot, core)
    others = [device_at((plane - 1 - step + 2 * planes) % planes, spot, core) for step in range(planes - 1)]
    has_before, has_after = plane > 0, plane < planes - 1
    offset = 1 - core
    per_block = prepared_ref.shape[2] // wide

    def loads(head):
        buf = head % 2
        wide_cut = pl.ds(pl.multiple_of(head * wide, 128), wide)
        return [
            pltpu.make_async_copy(
                held_ref.at[:, :, :, pl.ds(pl.multiple_of(head * HEAD_SIZE, 128), HEAD_SIZE)],
                held_buf.at[buf], load_sem.at[buf, 0],
            ),
            pltpu.make_async_copy(
                prepared_ref.at[head // per_block, :, pl.ds(pl.multiple_of(head % per_block * wide, 128), wide)],
                query_buf.at[buf], load_sem.at[buf, 1],
            ),
            pltpu.make_async_copy(
                weight_ref.at[:, wide_cut],
                weight_buf.at[buf], load_sem.at[buf, 2],
            ),
            pltpu.make_async_copy(high_ref.at[:, wide_cut], high_buf.at[buf], load_sem.at[buf, 3]),
            pltpu.make_async_copy(raw_ref.at[:, wide_cut], raw_buf.at[buf], load_sem.at[buf, 4]),
        ]

    for copy in loads(0):
        copy.start()
    keys_copy = pltpu.make_async_copy(
        raw_ref.at[:, pl.ds(QUERY_HEADS * HEAD_SIZE, heads * HEAD_SIZE)], raw_keys, keys_sem
    )
    keys_copy.start()
    greet([sibling] + mates + others)

    targets = [(plane + 1 + step) % planes for step in range(planes)]
    far_device = device_at(plane, first_and_second(spot, core)[1], core)

    def far_copy(step):
        return remote(
            kept_own.at[1, targets[step]], got_far.at[targets[step]], f_send.at[step], f_recv.at[step], far_device
        )

    def passed_copy(step):
        target = (plane - 1 - step + 2 * planes) % planes
        return remote(passed.at[target], got_passed.at[step], r_send.at[step], r_recv.at[step], others[step])

    def add_far(step):
        target = targets[step]
        far_copy(step).wait_recv()
        both = kept_own[0, target].astype(jnp.float32) + kept_got[0, target].astype(jnp.float32)
        both += got_far[target].astype(jnp.float32)
        if step == planes - 1:
            swap_out[...] = both
        else:
            passed[target] = both.astype(jnp.bfloat16)
            passed_copy(planes - 2 - step).start()

    def core_copy(head):
        return remote(sending.at[head % 2], theirs.at[head], c_send.at[head], c_recv.at[head], sibling)

    def mate_copy(index, head, hops):
        return remote(
            mine.at[head, hops], in_plane.at[index, head], p_send.at[index, head], p_recv.at[index, head], mates[index]
        )

    def z_copy(head):
        return remote(back.at[head], later.at[head], z_send.at[head], z_recv.at[head], before_device)

    def whole_copy(step):
        target = (plane - 1 - step + 2 * planes) % planes
        return remote(whole_ref.at[target], got_whole.at[step], v_send.at[step], v_recv.at[step], others[step])

    for step in range(planes - 1):
        whole_copy(step).start()
    whole_load = pltpu.make_async_copy(whole_ref.at[plane], whole_own, own_sem.at[2])
    whole_load.start()
    kept_loads = [
        pltpu.make_async_copy(kept_ref, kept_own, own_sem.at[0]),
        pltpu.make_async_copy(arrived_ref, kept_got, own_sem.at[1]),
    ]
    for copy in kept_loads:
        copy.start()

    def on_chip(head):
        core_copy(head).wait_recv()
        for index in range(HOPS):
            both = mine[head, index + core].astype(jnp.float32) + theirs[head, index].astype(jnp.float32)
            mine[head, index + core] = both.astype(jnp.bfloat16)
        for index in range(3):
            earlier = spots[index] < spot

            @pl.when(earlier | has_before)
            def _():
                mate_copy(index, head, spot - spots[index] + jnp.where(earlier, 0, 4)).start()

    def work(head):
        buf = head % 2
        for copy in loads(head):
            copy.wait()

        @pl.when(head + 1 < heads)
        def _():
            for copy in loads(head + 1):
                copy.start()

        low_grad = jnp.dot(branch_ref[...], weight_buf[buf], preferred_element_type=jnp.float32).astype(jnp.bfloat16)
        shared = low_grad.astype(jnp.float32) * high_buf[buf]
        for group in range(groups):
            rows = slice(group * tokens, (group + 1) * tokens)
            cut = slice(group * HEAD_SIZE, (group + 1) * HEAD_SIZE)
            grad_ref[rows] = low_grad[:, cut]
            stack_ref[rows] = query_buf[buf, :, cut]
            delta_ref[:, rows] = jnp.sum(shared[:, cut].T, axis=0, keepdims=True)
        sum_ref[...] = jnp.zeros(sum_ref.shape, jnp.float32)

        def blocks(slot, count):
            keys = held_blocks(held_buf.at[buf], offset + slot, count, 0)
            values = held_blocks(held_buf.at[buf], offset + slot, count, 1)
            query, grad = stack_ref[...], grad_ref[...]
            weights = jnp.exp2(contract_last(keys, query) * (scale * log2_e) - log_ref[head])
            own = None
            if count == 1:
                own = lax.broadcasted_iota(jnp.int32, weights.shape, 1)
                own = own - jnp.where(own >= tokens, tokens, 0)
            allowed = allowed_keys(weights.shape, 0, start_ref[...], slot + count - 1, tokens, own)
            weights = jnp.where(allowed, weights, 0.0)
            change = contract_last(values, grad) - delta_ref[...]
            low_scores = (weights * change).astype(jnp.bfloat16)
            value_grad = jnp.dot(weights.astype(jnp.bfloat16), grad, preferred_element_type=jnp.float32)
            key_grad = jnp.dot(low_scores, query, preferred_element_type=jnp.float32) * scale
            sum_ref[...] += contract_first(keys, low_scores)
            return key_grad.astype(jnp.bfloat16), value_grad.astype(jnp.bfloat16)

        key_grad, value_grad = blocks(0, 1)
        mine[head, 0, 0] = key_grad
        mine[head, 0, 1] = value_grad

        @pl.when(head > 1)
        def _():
            core_copy(head - 2).wait_send()

        @pl.when(head > 0)
        def _():
            on_chip(head - 1)

        def pair(index, carry):
            key_grad, value_grad = blocks(2 * index + 1, 2)
            mine[head, index + 1, 0] = key_grad[:tokens]
            mine[head, index + 1, 1] = value_grad[:tokens]
            sending[buf, index, 0] = key_grad[tokens:]
            sending[buf, index, 1] = value_grad[tokens:]
            return carry

        lax.fori_loop(0, HOPS, pair, 0)
        core_copy(head).start()
        for group in range(groups):
            cut = slice(group * HEAD_SIZE, (group + 1) * HEAD_SIZE)
            raw_grad, gain_grad = head_back(
                (sum_ref[:, group * tokens : (group + 1) * tokens] * scale).T, raw_buf[buf, :, cut], head_gain_ref[0],
                wave_ref[0], wave_ref[1],
            )
            out_cut = pl.ds(pl.multiple_of(head * wide + group * HEAD_SIZE, 128), HEAD_SIZE)
            query_out[:, out_cut] = raw_grad.astype(jnp.bfloat16)
            query_gain_ref[...] += gain_grad

    def on_plane(head):
        total[head] = mine[head, 0].astype(jnp.float32)
        for index in range(3):
            after_us = spots[index] > spot

            @pl.when(after_us | has_before)
            def _():
                mate_copy(index, head, 0).wait_recv()

            @pl.when(after_us)
            def _():
                total[head] += in_plane[index, head].astype(jnp.float32)

        @pl.when(has_before)
        def _():
            summed = mine[head, HOPS].astype(jnp.float32)
            for index in range(3):
                summed += jnp.where(spots[index] < spot, in_plane[index, head].astype(jnp.float32), 0.0)
            back[head] = summed.astype(jnp.bfloat16)
            z_copy(head).start()

    def finish(head):
        @pl.when(has_after)
        def _():
            z_copy(head).wait_recv()
            total[head] += later[head].astype(jnp.float32)

        cut = pl.ds(pl.multiple_of(head * HEAD_SIZE, 128), HEAD_SIZE)
        raw_grad, gain_grad = head_back(total[head, 0], raw_keys[:, cut], head_gain_ref[1], wave_ref[0], wave_ref[1])
        key_out[:, cut] = raw_grad.astype(jnp.bfloat16)
        value_cut = pl.ds(pl.multiple_of((heads + head) * HEAD_SIZE, 128), HEAD_SIZE)
        key_out[:, value_cut] = total[head, 1].astype(jnp.bfloat16)
        key_gain_ref[...] += gain_grad

    query_gain_ref[...] = jnp.zeros(query_gain_ref.shape, jnp.float32)
    key_gain_ref[...] = jnp.zeros(key_gain_ref.shape, jnp.float32)
    keys_copy.wait()

    plane_lag, finish_lag = 3, 5

    def turn(head, carry):
        work(head)

        @pl.when(head == 0)
        def _():
            for copy in kept_loads:
                copy.wait()
            for step in range(planes):
                target = targets[step]
                both = kept_own[1, target].astype(jnp.float32) + kept_got[1, target].astype(jnp.float32)
                kept_own[1, target] = both.astype(jnp.bfloat16)
                far_copy(step).start()

        for step in range(planes):

            @pl.when(head == 2 + 4 * step // planes)
            def _():
                add_far(step)

        @pl.when(head >= plane_lag)
        def _():
            on_plane(head - plane_lag)

        @pl.when(head >= finish_lag)
        def _():
            finish(head - finish_lag)

        return carry

    lax.fori_loop(0, heads, turn, 0)
    on_chip(heads - 1)
    for head in range(heads - plane_lag, heads):
        on_plane(head)
    whole_load.wait()
    for step in range(planes - 1):
        whole_copy(step).wait_recv()
    for there in range(4):
        summed = whole_own[there].astype(jnp.float32)
        for step in range(planes - 1):
            summed += got_whole[step, there].astype(jnp.float32)
        whole_out[there] = summed.astype(jnp.bfloat16)
    for step in range(planes - 1):
        passed_copy(step).wait_recv()
        swap_out[...] += got_passed[step].astype(jnp.float32)
    rows = swap_in.shape[0]
    swap = remote(swap_out.at[pl.ds(pl.multiple_of((1 - core) * rows, 8), rows)], swap_in, s_send, s_recv, sibling)
    swap.start()
    kept_out[core] = swap_out[pl.ds(pl.multiple_of(core * rows, 8), rows)]
    for head in range(heads - finish_lag, heads):
        finish(head)
    swap.wait_recv()
    kept_out[1 - core] = swap_in[...]
    swap.wait_send()
    for step in range(planes):
        far_copy(step).wait_send()
    for step in range(planes - 1):
        passed_copy(step).wait_send()
        whole_copy(step).wait_send()
    core_copy(heads - 2).wait_send()
    core_copy(heads - 1).wait_send()
    for head in range(heads):

        @pl.when(has_before)
        def _():
            z_copy(head).wait_send()

        for index in range(3):

            @pl.when((spots[index] < spot) | has_before)
            def _():
                mate_copy(index, head, 0).wait_send()


def attend_back(prepared, held, others_low, high, raw, kept, arrived, whole, start_row, branch, logs, wave, head_gains, devices):
    planes = devices // 8
    heads, groups = KEY_VALUE_HEADS, QUERY_HEADS // KEY_VALUE_HEADS
    tokens = prepared.shape[1]
    wide = groups * HEAD_SIZE
    rows, kept_columns = kept.shape[2:]
    kept_block = (rows, kept_columns)
    others = max(planes - 1, 1)
    low, high_type = jnp.bfloat16, jnp.float32
    sems = pltpu.SemaphoreType.DMA
    in_vmem = pl.BlockSpec(memory_space=pltpu.VMEM)
    in_any = pl.BlockSpec(memory_space=pl.ANY)
    part = (2, tokens, HEAD_SIZE)
    gain_row = jax.ShapeDtypeStruct((1, HEAD_SIZE), high_type)
    return pl.pallas_call(
        functools.partial(attend_back_kernel, planes),
        in_specs=[in_any] * 8 + [in_vmem] * 5,
        out_specs=[in_vmem] * 6,
        out_shape=[
            jax.ShapeDtypeStruct((tokens, QUERY_HEADS * HEAD_SIZE), low),
            jax.ShapeDtypeStruct((tokens, 2 * heads * HEAD_SIZE), low),
            gain_row,
            gain_row,
            jax.ShapeDtypeStruct((2, rows // 2, kept_columns), high_type),
            jax.ShapeDtypeStruct(whole.shape[1:], low),
        ],
        scratch_shapes=[
            pltpu.VMEM((2, SLOTS) + part, low),
            pltpu.VMEM((2, tokens, wide), low),
            pltpu.VMEM((2, others_low.shape[0], wide), low),
            pltpu.VMEM((2, tokens, wide), high_type),
            pltpu.VMEM((2, tokens, wide), high_type),
            pltpu.VMEM((tokens, heads * HEAD_SIZE), high_type),
            pltpu.VMEM((HEAD_SIZE, groups * tokens), high_type),
            pltpu.VMEM((groups * tokens, HEAD_SIZE), low),
            pltpu.VMEM((groups * tokens, HEAD_SIZE), low),
            pltpu.VMEM((1, groups * tokens), high_type),
            pltpu.VMEM((heads, HOPS + 1) + part, low),
            pltpu.VMEM((2, HOPS) + part, low),
            pltpu.VMEM((heads, HOPS) + part, low),
            pltpu.VMEM((3, heads) + part, low),
            pltpu.VMEM((heads,) + part, low),
            pltpu.VMEM((heads,) + part, low),
            pltpu.VMEM((heads,) + part, high_type),
            pltpu.VMEM((2, planes) + kept_block, low),
            pltpu.VMEM((2, planes) + kept_block, low),
            pltpu.VMEM((planes,) + kept_block, low),
            pltpu.VMEM((planes,) + kept_block, low),
            pltpu.VMEM((others,) + kept_block, low),
            pltpu.VMEM(whole.shape[1:], low),
            pltpu.VMEM((others,) + whole.shape[1:], low),
            pltpu.VMEM(kept_block, high_type),
            pltpu.VMEM((rows // 2, kept_columns), high_type),
            sems((2, 5)),
            sems,
            sems((heads,)),
            sems((heads,)),
            sems((3, heads)),
            sems((3, heads)),
            sems((heads,)),
            sems((heads,)),
            sems((3,)),
            sems((planes,)),
            sems((planes,)),
            sems((others,)),
            sems((others,)),
            sems((others,)),
            sems((others,)),
            sems,
            sems,
        ],
        compiler_params=pltpu.CompilerParams(
            collective_id=2, has_side_effects=True, vmem_limit_bytes=60 * 1024 * 1024
        ),
        cost_estimate=pl.CostEstimate(
            flops=20 * tokens * tokens * SLOTS * HEAD_SIZE * QUERY_HEADS, bytes_accessed=40 * 2**20, transcendentals=0
        ),
        name="attend_back",
    )(prepared, held, others_low, high, raw, kept, arrived, whole, start_row, branch, logs, wave, head_gains)


def project_kernel(input_ref, gain_ref, weight_ref, head_gain_ref, wave_ref, normed_ref, raw_ref, prepared_ref):
    tile = prepared_ref.shape[-1]
    step = pl.program_id(0)
    query_steps = QUERY_HEADS * HEAD_SIZE // tile
    key_steps = KEY_VALUE_HEADS * HEAD_SIZE // tile

    @pl.when(step == 0)
    def _():
        normed_ref[...] = rms_scale(input_ref[...].astype(jnp.float32), gain_ref[...]).astype(jnp.bfloat16)

    projected = jnp.dot(normed_ref[...], weight_ref[...], preferred_element_type=jnp.float32)

    @pl.when(step < query_steps + key_steps)
    def _():
        raw_ref[...] = projected
        for head in range(tile // HEAD_SIZE):
            cut = slice(head * HEAD_SIZE, (head + 1) * HEAD_SIZE)
            turned = head_forward(projected[:, cut], head_gain_ref[0], wave_ref[0], wave_ref[1])
            prepared_ref[:, cut] = turned.astype(jnp.bfloat16)

    @pl.when(step >= query_steps + key_steps)
    def _():
        prepared_ref[...] = projected.astype(jnp.bfloat16)


def project(residual_in, mixer_gain, weights, head_gains, wave):
    tokens, width = residual_in.shape
    block = KEY_VALUE_HEADS * HEAD_SIZE
    tile = 512
    per_block = block // tile
    query_steps = QUERY_HEADS * HEAD_SIZE // tile
    raw_steps = query_steps + per_block
    steps = raw_steps + per_block

    def whole(array):
        return pl.BlockSpec(array.shape, lambda step: (0,) * array.ndim)

    return pl.pallas_call(
        project_kernel,
        grid=(steps,),
        in_specs=[
            whole(residual_in),
            whole(mixer_gain),
            pl.BlockSpec((width, tile), lambda step: (0, step)),
            pl.BlockSpec((1, 1, HEAD_SIZE), lambda step: (jnp.where(step < query_steps, 0, 1), 0, 0)),
            whole(wave),
        ],
        out_specs=[
            whole(residual_in),
            pl.BlockSpec((tokens, tile), lambda step: (0, jnp.minimum(step, raw_steps - 1))),
            pl.BlockSpec((None, tokens, tile), lambda step: (step // per_block, 0, step % per_block)),
        ],
        out_shape=[
            jax.ShapeDtypeStruct((tokens, width), jnp.bfloat16),
            jax.ShapeDtypeStruct((tokens, raw_steps * tile), jnp.float32),
            jax.ShapeDtypeStruct((steps // per_block, tokens, block), jnp.bfloat16),
        ],
        compiler_params=pltpu.CompilerParams(vmem_limit_bytes=vmem_bytes),
        cost_estimate=pl.CostEstimate(
            flops=2 * tokens * width * steps * tile, bytes_accessed=20 * 2**20, transcendentals=0
        ),
        name="project",
    )(residual_in, mixer_gain, weights, head_gains, wave)


ff_tile = 256


def feed_forward_kernel(planes, half, *refs):
    if half == 0:
        input_ref, cotangent_ref, attended_ref, gain_ref, others_ref, *refs = refs
        normed_ref, middle_ref, total_ref, back_ref, sent_ref, kept_ref, *refs = refs
        out_weight, weight_sem, *refs = refs
    else:
        normed_ref, cotangent_ref, attended_any, middle_ref, total_in, back_in, gain_ref, others_ref, *refs = refs
        output_ref, grad_middle_ref, branch_ref, gain_grad_ref, sent_ref, kept_ref, whole_ref, *refs = refs
        total_ref, back_ref, *refs = refs
    (tiles, turned, their_left, right, give_grads, give_hidden,
     tile_sem, x_send, x_recv, g_send, g_recv, h_send, h_recv, own_sem) = refs
    plane, spot, core = place_of(lax.axis_index("dp"))
    near, far = first_and_second(spot, core)
    sibling = device_at(plane, spot, 1 - core)
    tokens = normed_ref.shape[0]
    units = give_grads.shape[1]
    steps = units // ff_tile
    first = QUERY_HEADS * HEAD_SIZE // ff_tile
    block_rows = sent_ref.shape[2]
    ours, theirs = pl.ds(0, tokens), pl.ds(tokens, tokens)

    def loads(step):
        buf = step % 2
        return [
            pltpu.make_async_copy(
                others_ref.at[
                    :, pl.ds(pl.multiple_of((first + (2 * part + half) * steps + step) * ff_tile, 128), ff_tile)
                ],
                tiles.at[buf, part], tile_sem.at[buf, part],
            )
            for part in range(3)
        ]

    if half == 0:
        weight_load = pltpu.make_async_copy(others_ref.at[:, pl.ds(0, out_weight.shape[1])], out_weight, weight_sem)
        weight_load.start()
    for copy in loads(0):
        copy.start()
    greet([sibling])

    def left_copy(index, source):
        return remote(source, their_left.at[index], x_send.at[index], x_recv.at[index], sibling)

    left_copy(1, cotangent_ref).start()
    if half == 0:
        weight_load.wait()
        middle = input_ref[...].astype(jnp.float32) + contract_last(attended_ref[...], out_weight[...])
        middle_ref[...] = middle
        normed_ref[...] = rms_scale(middle, gain_ref[...]).astype(jnp.bfloat16)
        total_ref[...] = jnp.zeros(total_ref.shape, jnp.float32)
        back_ref[...] = jnp.zeros(back_ref.shape, jnp.float32)
    else:
        columns = attended_any.shape[1] // 2
        out_cut = pl.ds(units + units // 2, columns)

        def attended_half(side):
            return attended_any.at[:, pl.ds(pl.multiple_of(side * columns, 128), columns)]

        attended_copy = remote(
            attended_half(1 - core), right.at[theirs, out_cut], x_send.at[3], x_recv.at[3], sibling
        )
        attended_copy.start()
        attended_own = pltpu.make_async_copy(attended_half(core), right.at[ours, out_cut], own_sem)
        attended_own.start()
        total_ref[...] = total_in[...]
        back_ref[...] = back_in[...]
    left_copy(0, normed_ref).start()

    def grads_copy(step):
        cut = pl.ds(pl.multiple_of(step * ff_tile, 128), ff_tile)
        return remote(give_grads.at[:, cut], right.at[theirs, cut], g_send.at[step], g_recv.at[step], sibling)

    def hidden_copy(step):
        cut = pl.ds(pl.multiple_of(step * ff_tile, 128), ff_tile)
        there = pl.ds(pl.multiple_of(units + step * ff_tile, 128), ff_tile)
        return remote(give_hidden.at[:, cut], right.at[theirs, there], h_send.at[step], h_recv.at[step], sibling)

    def tile(step, carry):
        buf = step % 2
        for copy in loads(step):
            copy.wait()

        @pl.when(step + 1 < steps)
        def _():
            for copy in loads(step + 1):
                copy.start()

        normed = normed_ref[...]
        gate_pre = jnp.dot(normed, tiles[buf, 0], preferred_element_type=jnp.float32)
        up_act = jnp.dot(normed, tiles[buf, 1], preferred_element_type=jnp.float32)
        grad_hidden = jnp.dot(cotangent_ref[...], tiles[buf, 2], preferred_element_type=jnp.float32)
        passing = 1.0 / (1.0 + jnp.exp(-gate_pre))
        activated = gate_pre * passing
        hidden = (activated * up_act).astype(jnp.bfloat16)
        slope = passing + activated * (1.0 - passing)
        grad_gate = (grad_hidden * up_act * slope).astype(jnp.bfloat16)
        grad_up = (grad_hidden * activated).astype(jnp.bfloat16)
        total_ref[...] += contract_last(hidden, tiles[buf, 2])
        back_ref[...] += contract_last(grad_gate, tiles[buf, 0]) + contract_last(grad_up, tiles[buf, 1])
        cut = pl.ds(pl.multiple_of(step * ff_tile, 128), ff_tile)

        @pl.when(core == 0)
        def _():
            right[ours, cut] = grad_gate
            give_grads[:, cut] = grad_up

        @pl.when(core == 1)
        def _():
            right[ours, cut] = grad_up
            give_grads[:, cut] = grad_gate

        grads_copy(step).start()
        place = step % (steps // 2)

        @pl.when(step // (steps // 2) == core)
        def _():
            right[ours, pl.ds(pl.multiple_of(units + place * ff_tile, 128), ff_tile)] = hidden

        @pl.when(step // (steps // 2) != core)
        def _():
            give_hidden[:, pl.ds(pl.multiple_of(place * ff_tile, 128), ff_tile)] = hidden
            hidden_copy(place).start()

        return carry

    lax.fori_loop(0, steps, tile, 0)
    if half == 1:
        middle = middle_ref[...]
        part, gain_grad = norm_back(back_ref[...], middle, gain_ref[...])
        grad_middle = cotangent_ref[...].astype(jnp.float32) + part
        grad_middle_ref[...] = grad_middle
        branch_ref[...] = grad_middle.astype(jnp.bfloat16)
        gain_grad_ref[...] = gain_grad
        left_copy(2, branch_ref).start()
        output_ref[...] = (middle + total_ref[...]).astype(jnp.bfloat16)

    def turn(index, own):
        turned[:, :, :, :tokens] = own[...].T.reshape(planes, 4, block_rows, tokens)
        left_copy(index, own).wait_recv()
        turned[:, :, :, tokens:] = their_left[index].T.reshape(planes, 4, block_rows, tokens)

    def form(start, columns):
        width = 512 if columns % 512 == 0 else 256

        def one(step, carry):
            cut = pl.ds(pl.multiple_of(start + step * width, 128), width)
            both = right[:, cut]
            for out_ref, spots in ((sent_ref, (near, across(spot, 3))), (kept_ref, (spot, far))):
                left = jnp.concatenate(
                    [turned[:, there].reshape(planes * block_rows, 2 * tokens) for there in spots], axis=0
                )
                product = jnp.dot(left, both, preferred_element_type=jnp.float32)
                out_ref[:, :, :, cut] = product.astype(jnp.bfloat16).reshape(2, planes, block_rows, width)
            return carry

        lax.fori_loop(0, columns // width, one, 0)

    turn(0, normed_ref)
    for step in range(steps):
        grads_copy(step).wait_recv()
    form(0, units)
    turn(1, cotangent_ref)
    for step in range(steps // 2):
        hidden_copy(step).wait_recv()
    form(units, units // 2)
    if half == 1:
        turn(2, branch_ref)
        attended_own.wait()
        attended_copy.wait_recv()
        width = 512

        def whole(step, carry):
            both = right[:, pl.ds(pl.multiple_of(units + units // 2 + step * width, 128), width)]
            cut = pl.ds(pl.multiple_of(step * width, 128), width)
            for part in range(2):
                group = slice(part * planes // 2, (part + 1) * planes // 2)
                left = turned[group].reshape(2 * planes * block_rows, 2 * tokens)
                product = jnp.dot(left, both, preferred_element_type=jnp.float32)
                whole_ref[group, :, :, cut] = product.astype(jnp.bfloat16).reshape(planes // 2, 4, block_rows, width)
            return carry

        lax.fori_loop(0, columns // width, whole, 0)
        left_copy(2, branch_ref).wait_send()
        attended_copy.wait_send()
    left_copy(0, normed_ref).wait_send()
    left_copy(1, cotangent_ref).wait_send()
    for step in range(steps):
        grads_copy(step).wait_send()
    for step in range(steps // 2):
        hidden_copy(step).wait_send()


def feed_forward(half, operands, others_low, devices, identity):
    planes = devices // 8
    tokens, width = operands[0].shape
    block_rows = 2 * width // devices
    units = FF // 2
    steps = units // ff_tile
    out_columns = QUERY_HEADS * HEAD_SIZE
    low, high = jnp.bfloat16, jnp.float32
    lows, highs = jax.ShapeDtypeStruct((tokens, width), low), jax.ShapeDtypeStruct((tokens, width), high)
    products = jax.ShapeDtypeStruct((2, planes, block_rows, units + units // 2), low)
    sems = pltpu.SemaphoreType.DMA
    in_vmem, in_any = pl.BlockSpec(memory_space=pltpu.VMEM), pl.BlockSpec(memory_space=pl.ANY)
    columns = units + units // 2
    if half == 0:
        in_specs = [in_vmem] * 4 + [in_any]
        out_shape = [lows, highs, highs, highs, products, products]
        scratch = [pltpu.VMEM((width, out_columns), low), sems]
    else:
        in_specs = [in_vmem] * 2 + [in_any] + [in_vmem] * 4 + [in_any]
        whole = jax.ShapeDtypeStruct((planes, 4, block_rows, out_columns // 2), low)
        out_shape = [lows, highs, lows, jax.ShapeDtypeStruct((1, width), high), products, products, whole]
        scratch = [pltpu.VMEM((tokens, width), high)] * 2
        columns += out_columns // 2
    return pl.pallas_call(
        functools.partial(feed_forward_kernel, planes, half),
        in_specs=in_specs,
        out_specs=[in_vmem] * len(out_shape),
        out_shape=out_shape,
        scratch_shapes=scratch
        + [
            pltpu.VMEM((2, 3, width, ff_tile), low),
            pltpu.VMEM((planes, 4, block_rows, 2 * tokens), low),
            pltpu.VMEM((3, tokens, width), low),
            pltpu.VMEM((2 * tokens, columns), low),
            pltpu.VMEM((tokens, units), low),
            pltpu.VMEM((tokens, units // 2), low),
            sems((2, 3)),
            sems((4,)),
            sems((4,)),
            sems((steps,)),
            sems((steps,)),
            sems((steps // 2,)),
            sems((steps // 2,)),
            sems,
        ],
        compiler_params=pltpu.CompilerParams(
            collective_id=identity, has_side_effects=True, vmem_limit_bytes=vmem_bytes
        ),
        cost_estimate=pl.CostEstimate(
            flops=10 * tokens * width * FF, bytes_accessed=30 * 2**20, transcendentals=0
        ),
        name="feed_forward_%d" % half,
    )(*operands, others_low)


def local(
    residual_in,
    cotangent,
    seq_lengths,
    mixer_master,
    mixer_moment,
    mixer_square,
    dense_master,
    dense_moment,
    dense_square,
    gains_master,
    gains_moment,
    gains_square,
):
    token_rows = residual_in.shape[0]
    devices = lax.axis_size("dp")
    device_index = lax.axis_index("dp")
    first_token = device_index * token_rows
    tokens = first_token + jnp.arange(token_rows, dtype=jnp.int32)
    segment, token_positions = segment_of(seq_lengths, tokens)
    start_row = (tokens - token_positions - first_token).astype(jnp.int32)
    needed = (token_rows - 1 - start_row[0]) // token_rows
    whole = jnp.maximum((-start_row[-1]) // token_rows, 0)
    start_row = jnp.concatenate([start_row] * (QUERY_HEADS // KEY_VALUE_HEADS))[None, :]

    gain_count = gains_master.shape[0]
    gain_rows = jnp.pad(
        gains_master[None, :], ((0, mixer_master.shape[0] - 1), (0, HEAD_SIZE - gain_count))
    )
    qkv_columns = (QUERY_HEADS + 2 * KEY_VALUE_HEADS) * HEAD_SIZE
    mixer_block = jnp.concatenate([mixer_master[:, :qkv_columns], gain_rows], axis=1).astype(jnp.bfloat16)
    gathered = gather_blocks(mixer_block, devices)
    mixer_low = gathered.reshape(MODEL_WIDTH, -1)
    gains_low = gathered[:, 0, qkv_columns : qkv_columns + gain_count].reshape(-1)
    other_block = jnp.concatenate([mixer_master[:, qkv_columns:], dense_master], axis=1).astype(jnp.bfloat16)
    other_block, gathered = lax.optimization_barrier((other_block, gathered))
    others_low = lax.all_gather(other_block, "dp", axis=0, tiled=True)
    gain_vector = gains_low.astype(jnp.float32)
    mixer_gain = gain_vector[None, :MODEL_WIDTH]
    dense_gain = gain_vector[None, MODEL_WIDTH : 2 * MODEL_WIDTH]
    head_gains = gain_vector[2 * MODEL_WIDTH :].reshape(2, 1, HEAD_SIZE)

    reach = jnp.max(jnp.abs(head_gains[0])) * jnp.max(jnp.abs(head_gains[1])) * (1.02 * log2_e * HEAD_SIZE**0.5)
    bounds = jnp.stack([1 - device_index % 2, whole, needed, reach < 60.0]).astype(jnp.int32)
    half_dim = HEAD_SIZE // 2
    inverse = rope_base ** (-jnp.arange(half_dim, dtype=jnp.float32) * 2.0 / HEAD_SIZE)
    angles = token_positions.astype(jnp.float32)[:, None] * inverse[None, :]
    cosine, sine = jnp.cos(angles), jnp.sin(angles)
    wave = jnp.stack([jnp.concatenate([cosine, cosine], axis=1), jnp.concatenate([-sine, sine], axis=1)])
    normed, raw, prepared = project(residual_in, mixer_gain, mixer_low, head_gains, wave)
    held = spread_keys(prepared, devices)
    attended, attended_high, log_sums = attend(bounds, prepared, held, start_row)
    normed_two, middle, total, back, first_sent, first_kept = feed_forward(
        0, (residual_in, cotangent, attended, dense_gain), others_low, devices, 3
    )
    first_arrived = to_near(first_sent, devices)
    block_output, grad_middle, grad_branch, grad_dense_gain, last_sent, last_kept, out_products = feed_forward(
        1, (normed_two, cotangent, attended, middle, total, back, dense_gain), others_low, devices, 5
    )
    last_arrived = to_near(last_sent, devices)
    grad_query_part, grad_key_part, grad_query_gain, grad_key_gain, first_halves, out_sum = attend_back(
        prepared,
        held,
        others_low,
        attended_high,
        raw,
        first_kept,
        first_arrived,
        out_products,
        start_row,
        grad_branch,
        log_sums,
        wave,
        head_gains,
        devices,
    )
    last_kept, grad_key_part = lax.optimization_barrier((last_kept, grad_key_part))
    gains_local = jnp.concatenate(
        [jnp.zeros((MODEL_WIDTH,), jnp.float32), grad_dense_gain[0], grad_query_gain[0], grad_key_gain[0]]
    )
    gains_size = gains_local.shape[0]
    padded = -(-gains_size // (8 * HEAD_SIZE)) * 8 * HEAD_SIZE
    gains_tile = jnp.pad(gains_local, (0, padded - gains_size)).reshape(-1, HEAD_SIZE)
    mixer_grad, last_halves, out_halves, residual_grad, gains_sum = last_gradients(
        normed,
        grad_query_part,
        grad_key_part,
        last_kept,
        last_arrived,
        out_sum,
        mixer_low,
        residual_in,
        mixer_gain,
        grad_middle,
        gains_tile,
        devices,
        4,
    )
    gains_grad = lax.dynamic_slice_in_dim(
        gains_sum.reshape(-1), device_index * gain_count, gain_count, 0
    )
    units = FF // 2
    ends = units, units + units // 2
    gate_up_parts = [halves[core][:, : ends[0]] for core in range(2) for halves in (first_halves, last_halves)]
    down_parts = [halves[core][:, ends[0] : ends[1]] for halves in (first_halves, last_halves) for core in range(2)]
    dense_grad = jnp.concatenate(gate_up_parts + down_parts, axis=1)
    mixer_grad = jnp.concatenate([mixer_grad, out_halves[0], out_halves[1]], axis=1)
    mixer_renewed, mixer_momentum, mixer_variance = adamw_update(
        mixer_master, mixer_moment, mixer_square, mixer_grad, rate_matrix, decay_weight
    )
    dense_renewed, dense_momentum, dense_variance = adamw_update(
        dense_master, dense_moment, dense_square, dense_grad, rate_matrix, decay_weight
    )
    gains_renewed, gains_momentum, gains_variance = adamw_update(
        gains_master, gains_moment, gains_square, gains_grad, rate_gains, 0.0
    )
    return (
        block_output,
        residual_grad,
        mixer_renewed,
        mixer_momentum,
        mixer_variance,
        dense_renewed,
        dense_momentum,
        dense_variance,
        gains_renewed,
        gains_momentum,
        gains_variance,
    )


def solution(mesh):
    return jax.shard_map(
        local,
        mesh=mesh,
        in_specs=(
            P("dp", None),
            P("dp", None),
            P(),
            P("dp", None),
            P("dp", None),
            P("dp", None),
            P("dp", None),
            P("dp", None),
            P("dp", None),
            P("dp"),
            P("dp"),
            P("dp"),
        ),
        out_specs=(
            P("dp", None),
            P("dp", None),
            P("dp", None),
            P("dp", None),
            P("dp", None),
            P("dp", None),
            P("dp", None),
            P("dp", None),
            P("dp"),
            P("dp"),
            P("dp"),
        ),
        check_vma=False,
    )
```
